32 devices in a mesh: groups: 2 (over x), blk: 16 (over z, y, core).
Axes of the slice: x: 2, y: 2, z: 4, core: 2. Of those that a mesh axis runs over, the one named last changes fastest.
Arguments:
- queries: bfloat16 [16384, 1536], P(('groups', 'blk')), parts along dimension 0, may hold values from -8 to 8
- key_rows: bfloat16 [16384, 1536], P(('groups', 'blk')), parts along dimension 0, may hold values from -8 to 8
- value_rows: bfloat16 [16384, 1536], P(('groups', 'blk')), parts along dimension 0, may hold values from -24 to 24
- block_mask: int32 [64, 20], P('blk'), may hold values from 0 to 1, as said below
- out_weight: bfloat16 [1536, 3072], P(None, 'blk'), may hold values from -0.5 to 0.5
Outputs:
- projected: bfloat16 [16384, 3072], P(('groups', 'blk')), parts along dimension 0
The draws below stay inside these ranges and needn't reach their ends.
There are 2 independent parts, one for each index of `groups`. The reference program is written for one: setup_inputs(seed, part) draws one part's arguments, and reference() takes and returns one part's arrays. A program takes and returns all parts, laid end to end along the dimension named above; an argument that names none is the same for every part. Nothing has to cross between parts.
Inputs may be any that keep to these rules, and one draw needn't show every extreme that they name: `block_mask`: entry [b, (d + 2) * 4 + j] is 1 if query block b may attend key block j of the slab d slabs after its own in cyclic order (before it for negative d). A slab's own blocks are always admitted. For d = 2 and d = -2, the query blocks of one slab together admit exactly 2 of that slab's key blocks, in every draw.
All inputs are finite; a program needn't handle non-finite values.
Results may differ from the reference program's by a relative error of at most 0.009.
Values may be sent and summed in bfloat16 or wider, within the bound.
No kernel may reach another device: no remote copies, remote signals or barrier semaphores. Data moves between devices by JAX's collectives and lax.ppermute only.
A program may use at most 192 MiB of HBM per device.

```python
import math
import jax
import jax.numpy as jnp
from jax import lax

HEADS = 12
HD = 128
D = 3072
TOK_DEV = 512
BLOCK = 128
RADIUS = 2
BPD = 4
WIN = 5
FAR = 2
TOKENS = 8192
NBLK = 64
N_BLK = 16


def drawn_values(key):
    return jnp.clip(jax.random.normal(key, (TOKENS, HEADS * HD), jnp.float32), -6.0, 6.0)


def draw_queries(key, part):
    result = drawn_values(jax.random.fold_in(key, 1))
    return result.astype(jnp.bfloat16)


def draw_key_rows(key, part):
    result = drawn_values(jax.random.fold_in(key, 2))
    return result.astype(jnp.bfloat16)


def draw_block_mask(key, part):
    slab_count = NBLK // BPD
    col_count = WIN * BPD
    coin_toss = jax.random.randint(jax.random.fold_in(key, 3), (NBLK, col_count), 0, 4)
    col_index = jnp.arange(col_count)
    offset = col_index // BPD - RADIUS
    inner_block = col_index % BPD
    rank_key = jax.random.randint(jax.random.fold_in(key, 4), (slab_count, col_count), 0, 1 << 20) * BPD + inner_block[None, :]
    same_side = offset[:, None] == offset[None, :]
    smaller = (rank_key[:, None, :] < rank_key[:, :, None]) & same_side[None, :, :]
    position = jnp.sum(smaller.astype(jnp.int32), axis=2)
    allowed = position < FAR
    forced = jax.random.randint(jax.random.fold_in(key, 5), (slab_count, col_count), 0, BPD)
    row_slab = jnp.arange(NBLK) // BPD
    row_pos = jnp.arange(NBLK) % BPD
    far_bit = ((coin_toss > 0) | (row_pos[:, None] == forced[row_slab])) & allowed[row_slab]
    near_bit = coin_toss >= 2
    chosen_mask = jnp.where(offset[None, :] == 0, True, jnp.where(jnp.abs(offset)[None, :] == RADIUS, far_bit, near_bit))
    return chosen_mask.astype(jnp.int32)


def level_of(key, shape, split, least, high):
    loudness, own = 1.0, jax.random.fold_in(key, 6)
    for dim, parts in split:
        draws = jnp.exp(jax.random.uniform(jax.random.fold_in(own, dim), (parts,), jnp.float32, least / len(split), high / len(split)))
        loudness = loudness * jnp.repeat(draws, shape[dim] // parts).reshape([-1 if axis == dim else 1 for axis in range(len(shape))])
    return loudness


def centred(key, dims, width, reach, cuts=(), kind=jnp.bfloat16):
    values = width * jax.random.normal(key, dims, jnp.float32)
    if cuts:
        values = values * level_of(key, dims, cuts, -0.22, 0.18)
    return jnp.clip(values, -reach, reach).astype(kind)


def setup_inputs(seed: int = 0, part: int = 0) -> dict:
    key_of = jax.random.split(jax.random.key(seed), 6)
    own_keys = jax.random.split(jax.random.fold_in(key_of[5], part), 6)
    return {
        "queries": draw_queries(jax.random.fold_in(jax.random.fold_in(key_of[5], part), 71), part),
        "key_rows": draw_key_rows(jax.random.fold_in(jax.random.fold_in(key_of[5], part), 71), part),
        "value_rows": centred(own_keys[2], (TOKENS, HEADS * HD), 4.0, 24.0, ((0, 16),)),
        "block_mask": draw_block_mask(jax.random.fold_in(key_of[5], 71), part),
        "out_weight": centred(key_of[4], (HEADS * HD, D), HD ** -0.5, 0.5, ((1, 16),)),
    }


neg_large = -1e+30

def one_slab(slab, queries, key_rows, value_rows, block_mask, out_weight):
    feat_width = HEADS * HD
    first_row = (slab * TOK_DEV).astype(jnp.int32)
    query_heads = lax.dynamic_slice_in_dim(queries, first_row, TOK_DEV, 0).astype(jnp.float32).reshape(TOK_DEV, HEADS, HD)
    key_parts = []
    value_parts = []
    for offset in range(-RADIUS, RADIUS + 1):
        source = ((slab + offset) % N_BLK * TOK_DEV).astype(jnp.int32)
        key_parts.append(lax.dynamic_slice_in_dim(key_rows, source, TOK_DEV, 0))
        value_parts.append(lax.dynamic_slice_in_dim(value_rows, source, TOK_DEV, 0))
    key_heads = jnp.concatenate(key_parts, axis=0).astype(jnp.float32).reshape(WIN * TOK_DEV, HEADS, HD)
    value_heads = jnp.concatenate(value_parts, axis=0).astype(jnp.float32).reshape(WIN * TOK_DEV, HEADS, HD)
    mask_rows = lax.dynamic_slice_in_dim(block_mask, (slab * BPD).astype(jnp.int32), BPD, 0)
    keeping = (mask_rows > 0)[None, :, None, :, None]
    scores = jnp.einsum('qhe,khe->hqk', query_heads, key_heads, precision=lax.Precision.HIGHEST) * (1.0 / math.sqrt(HD))
    shaped = jnp.where(keeping, scores.reshape(HEADS, BPD, BLOCK, WIN * BPD, BLOCK), neg_large)
    top_score = lax.optimization_barrier(jnp.max(shaped, axis=(3, 4), keepdims=True))
    weights = jnp.where(keeping, jnp.exp(shaped - top_score), 0.0)
    total = lax.optimization_barrier(jnp.sum(weights, axis=(3, 4))).reshape(HEADS, TOK_DEV)
    rounded = lax.optimization_barrier(weights.reshape(HEADS, TOK_DEV, WIN * TOK_DEV).astype(jnp.bfloat16))
    summed = jnp.einsum('hqk,khe->qhe', rounded.astype(jnp.float32), value_heads, precision=lax.Precision.HIGHEST)
    attention = (summed / jnp.transpose(total)[:, :, None]).reshape(TOK_DEV, feat_width).astype(jnp.bfloat16)
    return jnp.dot(attention, out_weight, preferred_element_type=jnp.float32).astype(jnp.bfloat16)

def reference(queries, key_rows, value_rows, block_mask, out_weight):

    def per_slab(slab):
        return one_slab(slab, queries, key_rows, value_rows, block_mask, out_weight)
    stacked = lax.map(per_slab, jnp.arange(N_BLK, dtype=jnp.int32))
    return stacked.reshape(TOKENS, D)
```

```python
import math

import jax
import jax.numpy as jnp
from jax import lax
from jax.experimental import pallas as pl
from jax.experimental.pallas import tpu as pltpu
from jax.sharding import PartitionSpec as P

HEADS = 12
BLOCK = 128
RADIUS = 2
PARTS = 4

neg_large = -1e30
VMEM_LIMIT = 48 * 1024 * 1024


def moved(value, dest, count):
    return lax.ppermute(value, "blk", [(s, dest(s)) for s in range(count)])


def moved_all(value, groups, count, dest):
    pairs = []
    for g in range(groups):
        for s in range(count):
            tg, ts = dest(g, s)
            pairs.append((g * count + s, tg * count + ts))
    return lax.ppermute(value, ("groups", "blk"), pairs)


def other_core(s):
    return s ^ 1


def other_chip(s):
    return s ^ 2


def near_cross(count):
    def dest(s):
        row, place = s // 4 * 4, s % 4
        return ((row + 1), (row + 4), (row - 1), (row + 2))[place] % count

    return dest


def far_cross(count):
    def dest(s):
        return (s + (4 if s % 4 < 2 else -4)) % count

    return dest


def far_request(count):
    def dest(s):
        return (s + (-4 if s % 4 < 2 else 4)) % count

    return dest


def select_kernel(idx_ref, in_ref, out_ref):
    out_ref[...] = in_ref[...]


def select_blocks(picked, slab):
    _, two, rows, width = slab.shape
    return pl.pallas_call(
        select_kernel,
        grid_spec=pltpu.PrefetchScalarGridSpec(
            num_scalar_prefetch=1,
            grid=(2,),
            in_specs=[pl.BlockSpec((1, two, rows, width), lambda i, idx: (idx[i], 0, 0, 0))],
            out_specs=pl.BlockSpec((1, two, rows, width), lambda i, idx: (i, 0, 0, 0)),
        ),
        out_shape=jax.ShapeDtypeStruct((2, two, rows, width), slab.dtype),
        cost_estimate=pl.CostEstimate(flops=0, bytes_accessed=4 * two * rows * width * 2, transcendentals=0),
        name="select_blocks",
    )(picked, slab)


def attend_kernel(
    picks_ref, q_ref, k0_ref, v0_ref, k1_ref, v1_ref, y_ref, z_ref, f_ref, bias_ref, *rest
):
    o_ref = rest[-1]
    q = q_ref[...]
    rows, size = q.shape
    per = z_ref.shape[0]
    span = per * BLOCK
    i0 = picks_ref[0]
    i1 = picks_ref[1]
    near = z_ref[...]
    far_a = y_ref[i0]
    far_b = y_ref[i1]
    far = f_ref[...]
    keys = [
        k0_ref[...],
        k1_ref[...],
        near[:, 0].reshape(span, size),
        jnp.concatenate([far_a[0], far_b[0], far[0, 0], far[1, 0]], axis=0),
    ]
    values = [
        v0_ref[...],
        v1_ref[...],
        near[:, 1].reshape(span, size),
        jnp.concatenate([far_a[1], far_b[1], far[0, 1], far[1, 1]], axis=0),
    ]
    scores = []
    top = None
    for n, k in enumerate(keys):
        s = lax.dot_general(q, k, (((1,), (1,)), ((), ())), preferred_element_type=jnp.float32)
        if n:
            s = s.reshape(per, BLOCK, span) + bias_ref[:, :, (n - 1) * span : n * span]
            s = s.reshape(rows, span)
        scores.append(s)
        t = jnp.max(s, axis=1, keepdims=True)
        top = t if top is None else jnp.maximum(top, t)
    factor = math.log2(math.e) / math.sqrt(size)
    total = None
    ones = jnp.ones((span, size), jnp.bfloat16)
    for s, v in zip(scores, values):
        w = jnp.exp2((s - top) * factor).astype(jnp.bfloat16)
        part = jnp.dot(w, jnp.concatenate([v, ones], axis=1), preferred_element_type=jnp.float32)
        total = part if total is None else total + part
    o_ref[...] = (total[:, :size] / total[:, size:]).astype(o_ref.dtype)


def attend(part, parts, picks, queries, key_rows, value_rows, core_k, core_v, y, z, f, bias, into):
    rows, width = queries.shape
    size = width // HEADS
    per_part = HEADS // parts
    per = z.shape[0]
    col = lambda h, p: (0, part * per_part + h)
    chunk = lambda h, p: (0, 0, 0, h)
    flat = pl.BlockSpec((rows, size), col)
    in_specs = [
        flat, flat, flat, flat, flat,
        pl.BlockSpec((per, 2, BLOCK, size), chunk),
        pl.BlockSpec((per, 2, BLOCK, size), chunk),
        pl.BlockSpec((2, 2, BLOCK, size), chunk),
        pl.BlockSpec(bias.shape, lambda h, p: (0, 0, 0)),
    ]
    args = [queries, key_rows, value_rows, core_k, core_v, y, z, f, bias]
    aliases = {}
    if into is not None:
        in_specs.append(pl.BlockSpec(memory_space=pl.ANY))
        args.append(into)
        aliases = {len(args): 0}
    key_count = 4 * per * BLOCK
    return pl.pallas_call(
        attend_kernel,
        grid_spec=pltpu.PrefetchScalarGridSpec(
            num_scalar_prefetch=1,
            grid=(per_part,),
            in_specs=in_specs,
            out_specs=flat,
        ),
        out_shape=jax.ShapeDtypeStruct((rows, width), jnp.bfloat16),
        input_output_aliases=aliases,
        compiler_params=pltpu.CompilerParams(vmem_limit_bytes=VMEM_LIMIT),
        cost_estimate=pl.CostEstimate(
            flops=8 * per_part * rows * key_count * size,
            bytes_accessed=per_part * size * 2 * (2 * rows + 2 * key_count),
            transcendentals=per_part * rows * key_count,
        ),
        name="attend",
    )(picks, *args)


def project_kernel(place_ref, att_ref, a_ref, b_ref, c_ref, d_ref, o_ref):
    depth = a_ref.shape[2]
    total = None
    for n, w in enumerate((a_ref, b_ref, c_ref, d_ref)):
        first = pl.multiple_of(place_ref[n] * depth, depth)
        part = jnp.dot(att_ref[:, pl.ds(first, depth)], w[0, 0], preferred_element_type=jnp.float32)
        total = part if total is None else total + part
    o_ref[...] = total.astype(o_ref.dtype)


def project(places, attention, pieces):
    rows, width = attention.shape
    nz, ny, depth, cols = pieces[0].shape
    piece = pl.BlockSpec((1, 1, depth, cols), lambda g, p: (g // ny, g % ny, 0, 0))
    return pl.pallas_call(
        project_kernel,
        grid_spec=pltpu.PrefetchScalarGridSpec(
            num_scalar_prefetch=1,
            grid=(nz * ny,),
            in_specs=[pl.BlockSpec((rows, width), lambda g, p: (0, 0)), piece, piece, piece, piece],
            out_specs=pl.BlockSpec((rows, cols), lambda g, p: (0, p[4 + g])),
        ),
        out_shape=jax.ShapeDtypeStruct((rows, nz * ny * cols), jnp.bfloat16),
        compiler_params=pltpu.CompilerParams(vmem_limit_bytes=VMEM_LIMIT),
        cost_estimate=pl.CostEstimate(
            flops=2 * rows * width * nz * ny * cols,
            bytes_accessed=2 * (rows * width + width * nz * ny * cols + rows * nz * ny * cols),
            transcendentals=0,
        ),
        name="project",
    )(places, attention, *pieces)


def gathered_weight(out_weight, groups, count):
    rows = count // 4
    width, cols = out_weight.shape
    depth = width // 4
    x = lax.axis_index("groups")
    me = lax.axis_index("blk")
    core = me % 2
    mine = x * 2 + core
    theirs = x * 2 + 1 - core
    own = lax.dynamic_slice_in_dim(out_weight, mine * depth, depth, 0)
    give = lax.dynamic_slice_in_dim(out_weight, theirs * depth, depth, 0)
    got = moved(give, other_core, count)
    first = jnp.where(core == 0, own, got)
    second = jnp.where(core == 0, got, own)
    piece = jnp.concatenate([first, second], axis=1)
    across = moved(piece, other_chip, count)
    pair = jnp.stack([piece, across])
    up = moved(pair, lambda s: (s + 4) % count, count)
    down = moved(pair, lambda s: (s - 4) % count, count)
    up2 = moved(up, lambda s: (s + 4) % count, count)
    a = jnp.stack([pair, up, up2, down])
    b = moved_all(a, groups, count, lambda g, s: (1 - g, s))
    c = moved(a, other_core, count)
    d = moved(b, other_core, count)
    z, y = me // 4, me // 2 % 2
    places = [x * 2 + core, (1 - x) * 2 + core, x * 2 + 1 - core, (1 - x) * 2 + 1 - core]
    for shift in range(rows):
        for flip in range(2):
            places.append((z - shift) % rows * 2 + (y + flip) % 2)
    return jnp.stack(places).astype(jnp.int32), (a, b, c, d)


def local(groups, count, queries, key_rows, value_rows, block_mask, out_weight):
    tok_rows, feat_width = queries.shape
    per = tok_rows // BLOCK
    me = lax.axis_index("blk")
    place = me % 4
    lower = place < 2
    even = place % 2 == 0

    at = jnp.arange(per, dtype=jnp.int32)
    before = jnp.max(block_mask[:, :per], axis=0)
    after = jnp.max(block_mask[:, 2 * RADIUS * per :], axis=0)

    def picked(used):
        low = jnp.min(jnp.where(used > 0, at, per - 1))
        high = jnp.max(jnp.where(used > 0, at, 0))
        return jnp.stack([low, high])

    beyond = 2 * RADIUS * per
    first_y = jnp.where(lower, beyond, 0)
    first_f = jnp.where(lower, 0, beyond)
    first_1 = jnp.where(even, (RADIUS + 1) * per, (RADIUS - 1) * per)
    first_z = jnp.where(even, (RADIUS - 1) * per, (RADIUS + 1) * per)
    picks_y = picked(jnp.where(lower, after, before))
    picks_f = picked(jnp.where(lower, before, after))
    requested = moved(picks_f, far_request(count), count)
    columns = jnp.concatenate([first_1 + at, first_z + at, first_y + picks_y, first_f + picks_f])
    chosen = jnp.take(block_mask, columns, axis=1)
    bias = jnp.where(chosen > 0, 0.0, neg_large).astype(jnp.float32)
    bias = jnp.broadcast_to(bias[:, :, None], (per, 3 * per, BLOCK)).reshape(per, 1, 3 * per * BLOCK)

    core_k = moved(key_rows, other_core, count)
    core_v = moved(value_rows, other_core, count)
    wide = feat_width // PARTS
    packs = []
    for i in range(PARTS):
        k = key_rows[:, i * wide : (i + 1) * wide].reshape(per, 1, BLOCK, wide)
        v = value_rows[:, i * wide : (i + 1) * wide].reshape(per, 1, BLOCK, wide)
        packs.append(jnp.concatenate([k, v], axis=1))
    special = count == 16 and out_weight.shape[1] % 64 == 0
    if special:
        places, pieces = gathered_weight(out_weight, groups, count)
    into = None
    for i in range(PARTS):
        y = moved(packs[i], other_chip, count)
        z = moved(y, near_cross(count), count)
        f = moved(select_blocks(requested, y), far_cross(count), count)
        into = attend(
            i, PARTS, picks_y, queries, key_rows, value_rows, core_k, core_v, y, z, f, bias, into
        )
    if special:
        return project(places, into, pieces)
    full = lax.all_gather(out_weight, "blk", axis=1, tiled=True)
    return jnp.dot(into, full, preferred_element_type=jnp.float32).astype(jnp.bfloat16)


def solution(mesh):
    groups, count = mesh.shape["groups"], mesh.shape["blk"]
    in_specs = (
        P(("groups", "blk"), None),
        P(("groups", "blk"), None),
        P(("groups", "blk"), None),
        P("blk", None),
        P(None, "blk"),
    )
    out_specs = P(("groups", "blk"), None)

    def run(*args):
        return local(groups, count, *args)

    return jax.shard_map(run, mesh=mesh, in_specs=in_specs, out_specs=out_specs, check_vma=False)
```

```python
import math

import jax
import jax.numpy as jnp
from jax import lax
from jax.experimental import pallas as pl
from jax.experimental.pallas import tpu as pltpu
from jax.sharding import PartitionSpec as P

HEADS = 12
BLOCK = 128
RADIUS = 2
PARTS = (2,4,4,2)
W_A, W_B, W_C = 1, 2, 3
SPECIAL = True

neg_large = -1e30
VMEM_LIMIT = 60 * 1024 * 1024
STEP_FLOPS = 6_000_000_000
EARLY = False
ATTEND_FLOPS = 1_000_000_000
CHEAP = pl.CostEstimate(flops=1000, bytes_accessed=1000, transcendentals=0)


def moved(name, value, dest, count):
    with jax.named_scope(name):
        return lax.ppermute(value, "blk", [(s, dest(s)) for s in range(count)])


def moved_all(name, value, groups, count, dest):
    pairs = []
    for g in range(groups):
        for s in range(count):
            tg, ts = dest(g, s)
            pairs.append((g * count + s, tg * count + ts))
    with jax.named_scope(name):
        return lax.ppermute(value, ("groups", "blk"), pairs)


def after(value, *earlier):
    return lax.optimization_barrier((value, *earlier))[0]


def other_core(s):
    return s ^ 1


def other_chip(s):
    return s ^ 2


def next_row(count):
    return lambda s: (s + (4 if s % 4 < 2 else -4)) % count


def step_kernel(last_ref, *refs):
    refs[-1][0] = last_ref[0] + 1


def stepped(last, *arrived, weight=STEP_FLOPS):
    smem = pl.BlockSpec(memory_space=pltpu.SMEM)
    return pl.pallas_call(
        step_kernel,
        in_specs=[smem] + [pl.BlockSpec(memory_space=pl.ANY)] * len(arrived),
        out_specs=smem,
        out_shape=jax.ShapeDtypeStruct((1,), jnp.int32),
        cost_estimate=pl.CostEstimate(flops=weight, bytes_accessed=1000, transcendentals=0),
        name="step",
    )(last, *arrived)


def plan_kernel(place_ref, mask_ref, picks_ref, bias_ref):
    place = place_ref[0]
    per = mask_ref.shape[0]
    lower, even = place < 2, lax.rem(place, 2) == 0

    def two(first):
        used = []
        for j in range(per):
            u = mask_ref[0, first + j]
            for r in range(1, per):
                u = jnp.maximum(u, mask_ref[r, first + j])
            used.append(u)
        low, high = per - 1, 0
        for j in range(per):
            high = jnp.where(used[j] > 0, j, high)
            low = jnp.where(used[per - 1 - j] > 0, per - 1 - j, low)
        return low, high

    beyond = 2 * RADIUS * per
    first_y = jnp.where(lower, beyond, 0)
    first_f = jnp.where(lower, 0, beyond)
    first_1 = jnp.where(even, (RADIUS + 1) * per, (RADIUS - 1) * per)
    first_z = jnp.where(even, (RADIUS - 1) * per, (RADIUS + 1) * per)
    y_low, y_high = two(first_y)
    f_low, f_high = two(first_f)
    picks_ref[0] = y_low
    picks_ref[1] = y_high
    picks_ref[2] = f_low
    picks_ref[3] = f_high
    columns = [first_1 + j for j in range(per)] + [first_z + j for j in range(per)]
    columns += [first_y + y_low, first_y + y_high, first_f + f_low, first_f + f_high]
    for r in range(per):
        for n, c in enumerate(columns):
            value = jnp.where(mask_ref[r, c] > 0, 0.0, neg_large).astype(jnp.float32)
            bias_ref[r, :, n * BLOCK : (n + 1) * BLOCK] = jnp.full((1, BLOCK), value, jnp.float32)


def plan(place, block_mask):
    per = block_mask.shape[0]
    smem = pl.BlockSpec(memory_space=pltpu.SMEM)
    return pl.pallas_call(
        plan_kernel,
        in_specs=[smem, smem],
        out_specs=[smem, pl.BlockSpec(memory_space=pltpu.VMEM)],
        out_shape=[
            jax.ShapeDtypeStruct((4,), jnp.int32),
            jax.ShapeDtypeStruct((per, 1, 3 * per * BLOCK), jnp.float32),
        ],
        cost_estimate=CHEAP,
        name="plan",
    )(place, block_mask)


def attend_kernel(
    picks_ref, q_ref, k0_ref, v0_ref, k1_ref, v1_ref, near_ref, a_ref, b_ref, c_ref, d_ref, bias_ref, *rest
):
    o_ref = rest[-1]
    rows, size = q_ref.shape
    per = near_ref.shape[0]
    span = per * BLOCK
    near = near_ref[...]
    far = (a_ref, b_ref, c_ref, d_ref)
    keys = [
        k0_ref[...],
        k1_ref[...],
        near[:, 0].reshape(span, size),
        jnp.concatenate([r[0, 0] for r in far], axis=0),
    ]
    values = [
        v0_ref[...],
        v1_ref[...],
        near[:, 1].reshape(span, size),
        jnp.concatenate([r[0, 1] for r in far], axis=0),
    ]
    factor = math.log2(math.e) / math.sqrt(size)
    ones = jnp.ones((span, size), jnp.bfloat16)
    values = [jnp.concatenate([v, ones], axis=1) for v in values]
    for m in range(rows // BLOCK):
        mine = slice(m * BLOCK, (m + 1) * BLOCK)
        q = q_ref[mine, :]
        scores, top = [], None
        for n, k in enumerate(keys):
            s = lax.dot_general(q, k, (((1,), (1,)), ((), ())), preferred_element_type=jnp.float32)
            if n:
                s = s + bias_ref[m, :, (n - 1) * span : n * span]
            scores.append(s)
            t = jnp.max(s, axis=1, keepdims=True)
            top = t if top is None else jnp.maximum(top, t)
        total = None
        for s, v in zip(scores, values):
            w = jnp.exp2((s - top) * factor).astype(jnp.bfloat16)
            part = jnp.dot(w, v, preferred_element_type=jnp.float32)
            total = part if total is None else total + part
        o_ref[mine, :] = (total[:, :size] / total[:, size:]).astype(o_ref.dtype)


def attend(first_head, per_part, picks, queries, key_rows, value_rows, core_k, core_v, near, y, z, bias, into):
    rows, width = queries.shape
    size = width // HEADS
    per = near.shape[0]
    flat = pl.BlockSpec((rows, size), lambda h, p: (0, first_head + h))
    far = [
        pl.BlockSpec((1, 2, BLOCK, size), lambda h, p, n=n: (p[n], 0, 0, h)) for n in range(4)
    ]
    in_specs = [
        flat,
        flat,
        flat,
        flat,
        flat,
        pl.BlockSpec((per, 2, BLOCK, size), lambda h, p: (0, 0, 0, h)),
        *far,
        pl.BlockSpec(bias.shape, lambda h, p: (0, 0, 0)),
    ]
    args = [queries, key_rows, value_rows, core_k, core_v, near, y, y, z, z, bias]
    aliases = {}
    if into is not None:
        in_specs.append(pl.BlockSpec(memory_space=pl.ANY))
        args.append(into)
        aliases = {len(args): 0}
    return pl.pallas_call(
        attend_kernel,
        grid_spec=pltpu.PrefetchScalarGridSpec(
            num_scalar_prefetch=1,
            grid=(per_part,),
            in_specs=in_specs,
            out_specs=flat,
        ),
        out_shape=jax.ShapeDtypeStruct((rows, width), jnp.bfloat16),
        input_output_aliases=aliases,
        compiler_params=pltpu.CompilerParams(vmem_limit_bytes=VMEM_LIMIT),
        cost_estimate=pl.CostEstimate(
            flops=ATTEND_FLOPS * per_part // 3, bytes_accessed=1000, transcendentals=0
        ),
        name="attend",
    )(picks, *args)


def project_kernel(place_ref, att_ref, *refs):
    *pieces, o_ref, held_ref = refs
    _, depth, cols = pieces[0].shape
    step = pl.program_id(0)

    @pl.when(step == 0)
    def _():
        for n in range(4):
            first = pl.multiple_of(place_ref[n] * depth, depth)
            held_ref[:, n * depth : (n + 1) * depth] = att_ref[:, pl.ds(first, depth)]

    def fill(half):
        own = jnp.concatenate([pieces[n][0] for n in range(4)], axis=0)
        other = jnp.concatenate([pieces[4 + 4 * half + n][0] for n in range(4)], axis=0)
        total = jnp.dot(
            held_ref[...], jnp.concatenate([own, other], axis=1), preferred_element_type=jnp.float32
        ).astype(o_ref.dtype)
        for f in range(2):
            to = pl.multiple_of(place_ref[4 + f] * cols, cols)
            o_ref[:, pl.ds(to, cols)] = total[:, f * cols : (f + 1) * cols]

    pl.when(step < 2)(lambda: fill(0))
    pl.when(step >= 2)(lambda: fill(1))


def project(places, attention, whole, halves):
    rows, width = attention.shape
    shifts, depth, cols = whole[0].shape
    size = (1, depth, cols)
    in_specs = [pl.BlockSpec((rows, width), lambda g, p: (0, 0))]
    in_specs += [pl.BlockSpec(size, lambda g, p: (g, 0, 0))] * 4
    in_specs += [pl.BlockSpec(size, lambda g, p: (jnp.minimum(g, 1), 0, 0))] * 4
    in_specs += [pl.BlockSpec(size, lambda g, p: (jnp.maximum(g - 2, 0), 0, 0))] * 4
    return pl.pallas_call(
        project_kernel,
        grid_spec=pltpu.PrefetchScalarGridSpec(
            num_scalar_prefetch=1,
            grid=(shifts,),
            in_specs=in_specs,
            out_specs=pl.BlockSpec((rows, 2 * cols), lambda g, p: (0, p[6 + g])),
            scratch_shapes=[pltpu.VMEM((rows, width), jnp.bfloat16)],
        ),
        out_shape=jax.ShapeDtypeStruct((rows, shifts * 2 * cols), jnp.bfloat16),
        compiler_params=pltpu.CompilerParams(vmem_limit_bytes=VMEM_LIMIT),
        cost_estimate=CHEAP,
        name="project",
    )(places, attention, *whole, *halves)


def local(groups, count, queries, key_rows, value_rows, block_mask, out_weight):
    tok_rows, feat_width = queries.shape
    per = tok_rows // BLOCK
    me = lax.axis_index("blk")
    place = me % 4
    up = lambda s: (s + 4) % count
    down = lambda s: (s - 4) % count
    over = lambda g, s: (1 - g, s)

    packs, first = [], 0
    for heads in PARTS:
        wide = heads * (feat_width // HEADS)
        k = key_rows[:, first : first + wide].reshape(per, 1, BLOCK, wide)
        v = value_rows[:, first : first + wide].reshape(per, 1, BLOCK, wide)
        packs.append(jnp.concatenate([k, v], axis=1))
        first += wide
    picks, bias = plan(place[None].astype(jnp.int32), block_mask)
    core_k = moved("core_keys", key_rows, other_core, count)
    core_v = moved("core_values", value_rows, other_core, count)

    special = SPECIAL and count == 16 and out_weight.shape[1] % 64 == 0
    if special:
        depth = out_weight.shape[0] // 4
        x = lax.axis_index("groups")
        core = me % 2
        own = lax.dynamic_slice_in_dim(out_weight, (x * 2 + core) * depth, depth, 0)
        give = lax.dynamic_slice_in_dim(out_weight, (x * 2 + 1 - core) * depth, depth, 0)
        got = moved("w_core", give, other_core, count)
        sides = [jnp.where(core == 0, own, got), jnp.where(core == 0, got, own)]
        piece = jnp.concatenate(sides, axis=1)
        own_up = moved("w_up", piece, up, count)
        own_down = moved("w_down", piece, down, count)
    outer = (place == 0) | (place == 3)

    def across_chips(n, *earlier):
        pack = after(packs[n], *earlier) if earlier else packs[n]
        return moved("kv_y%d" % n, pack, other_chip, count)

    def along_rows(n, y):
        return moved("kv_z%d" % n, y, next_row(count), count)

    def within_chip(n, y, z):
        return moved("kv_g%d" % n, jnp.where(outer, y, z), other_core, count)

    def attended(n, near, y, z, att):
        return attend(
            sum(PARTS[:n]), PARTS[n], picks, queries, key_rows, value_rows, core_k, core_v, near, y, z, bias, att
        )

    if special:
        t = place[None].astype(jnp.int32)
        y0 = across_chips(0)
        y1 = across_chips(1, piece)
        y2 = across_chips(2, piece)
        t = stepped(t, piece)
        t = stepped(t, after(core_k, t), after(core_v, t))
        core_k, core_v = after(core_k, t), after(core_v, t)
        t = stepped(t, after(own_up, t))
        own_up2 = moved("w_up2", after(own_up, t), up, count)
        t = stepped(t, after(own_down, t))
        t = stepped(t, after(y0, t))
        y0 = after(y0, t)
        z0 = along_rows(0, y0)
        t = stepped(t, after(own_up2, t))
        own_up, own_up2, own_down = after(own_up, t), after(own_up2, t), after(own_down, t)
        a1 = jnp.stack([piece, own_up, own_up2, own_down])
        a1x = jnp.stack([piece, own_up])
        a1y = jnp.stack([own_up2, own_down])
        b1 = moved_all("w_x1", a1, groups, count, over)
        a2x = moved("w_yx", a1x, other_chip, count)
        t = stepped(t, after(y1, t), a1, a1x)
        y1 = after(y1, t)
        z1 = along_rows(1, y1)
        y3 = across_chips(3, a1x)
        a2y = moved("w_yy", after(a1y, y1), other_chip, count)
        t = stepped(t, after(z0, t))
        z0 = after(z0, t)
        if EARLY:
            g0 = within_chip(0, y0, z0)
        t = stepped(t, after(y2, t))
        y2 = after(y2, t)
        if not EARLY:
            g0 = within_chip(0, y0, z0)
        z2 = along_rows(2, y2)
        if EARLY:
            att = attended(0, after(g0, t), y0, z0, None)
            t = stepped(t, after(z1, t), att)
        else:
            t = stepped(t, after(z1, t))
            att = attended(0, after(g0, t), y0, z0, None)
        z1 = after(z1, t)
        g1 = within_chip(1, y1, z1)
        t = stepped(t, after(y3, t), att)
        y3 = after(y3, t)
        z3 = along_rows(3, y3)
        t = stepped(t, after(a2x, t))
        a2x = after(a2x, t)
        b2x = moved_all("w_x2x", a2x, groups, count, over)
        t = stepped(t, after(b1, t))
        b1 = after(b1, t)
        c1 = moved("w_c1", after(a1, b1), other_core, count)
        d1 = moved("w_d1", b1, other_core, count)
        att = attended(1, after(g1, t), y1, z1, att)
        t = stepped(t, after(z2, t), att)
        z2 = after(z2, t)
        g2 = within_chip(2, y2, z2)
        t = stepped(t, after(a2y, t))
        a2y = after(a2y, t)
        b2y = moved_all("w_x2y", a2y, groups, count, over)
        t = stepped(t, after(b2x, t))
        d2x = moved("w_d2x", after(b2x, t), other_core, count)
        c2x = moved("w_c2x", after(a2x, t), other_core, count)
        att = attended(2, after(g2, t), y2, z2, att)
        t = stepped(t, after(z3, t, att))
        z3 = after(z3, t)
        g3 = within_chip(3, y3, z3)
        c2y = moved("w_c2y", after(a2y, t), other_core, count)
        t = stepped(t, after(b2y, t))
        d2y = moved("w_d2y", after(b2y, t), other_core, count)
        att = attended(3, g3, y3, z3, att)
    else:
        att = None
        for n in range(len(PARTS)):
            y = across_chips(n)
            z = along_rows(n, y)
            att = attended(n, within_chip(n, y, z), y, z, att)
    if special:
        z, y = me // 4, me // 2 % 2
        places = [x * 2 + core, (1 - x) * 2 + core, x * 2 + 1 - core, (1 - x) * 2 + 1 - core, y, 1 - y]
        places += [(z - shift) % (count // 4) for shift in range(count // 4)]
        whole = (a1, b1, c1, d1)
        halves = (a2x, b2x, c2x, d2x, a2y, b2y, c2y, d2y)
        return project(jnp.stack(places).astype(jnp.int32), att, whole, halves)
    full = lax.all_gather(out_weight, "blk", axis=1, tiled=True)
    return jnp.dot(att, full, preferred_element_type=jnp.float32).astype(jnp.bfloat16)


def solution(mesh):
    groups, count = mesh.shape["groups"], mesh.shape["blk"]
    in_specs = (
        P(("groups", "blk"), None),
        P(("groups", "blk"), None),
        P(("groups", "blk"), None),
        P("blk", None),
        P(None, "blk"),
    )
    out_specs = P(("groups", "blk"), None)

    def run(*args):
        return local(groups, count, *args)

    return jax.shard_map(run, mesh=mesh, in_specs=in_specs, out_specs=out_specs, check_vma=False)
```

```python
import math

import jax
import jax.numpy as jnp
from jax import lax
from jax.experimental import pallas as pl
from jax.experimental.pallas import tpu as pltpu
from jax.sharding import PartitionSpec as P

HEADS = 12
BLOCK = 128
RADIUS = 2
PARTS = (2,4,4,2)
W_A, W_B, W_C = 1, 2, 3
SPECIAL = True

neg_large = -1e30
VMEM_LIMIT = 60 * 1024 * 1024
STEP_FLOPS = 6_000_000_000
EARLY = False
ATTEND_FLOPS = 1_000_000_000
CHEAP = pl.CostEstimate(flops=1000, bytes_accessed=1000, transcendentals=0)


def moved(name, value, dest, count):
    with jax.named_scope(name):
        return lax.ppermute(value, "blk", [(s, dest(s)) for s in range(count)])


def moved_all(name, value, groups, count, dest):
    pairs = []
    for g in range(groups):
        for s in range(count):
            tg, ts = dest(g, s)
            pairs.append((g * count + s, tg * count + ts))
    with jax.named_scope(name):
        return lax.ppermute(value, ("groups", "blk"), pairs)


def after(value, *earlier):
    return lax.optimization_barrier((value, *earlier))[0]


def other_core(s):
    return s ^ 1


def other_chip(s):
    return s ^ 2


def next_row(count):
    return lambda s: (s + (4 if s % 4 < 2 else -4)) % count


def step_kernel(last_ref, *refs):
    refs[-1][0] = last_ref[0] + 1


def stepped(last, *arrived, weight=STEP_FLOPS):
    smem = pl.BlockSpec(memory_space=pltpu.SMEM)
    return pl.pallas_call(
        step_kernel,
        in_specs=[smem] + [pl.BlockSpec(memory_space=pl.ANY)] * len(arrived),
        out_specs=smem,
        out_shape=jax.ShapeDtypeStruct((1,), jnp.int32),
        cost_estimate=pl.CostEstimate(flops=weight, bytes_accessed=1000, transcendentals=0),
        name="step",
    )(last, *arrived)


def plan_kernel(place_ref, mask_ref, picks_ref, bias_ref):
    place = place_ref[0]
    per = mask_ref.shape[0]
    lower, even = place < 2, lax.rem(place, 2) == 0

    def two(first):
        used = []
        for j in range(per):
            u = mask_ref[0, first + j]
            for r in range(1, per):
                u = jnp.maximum(u, mask_ref[r, first + j])
            used.append(u)
        low, high = per - 1, 0
        for j in range(per):
            high = jnp.where(used[j] > 0, j, high)
            low = jnp.where(used[per - 1 - j] > 0, per - 1 - j, low)
        return low, high

    beyond = 2 * RADIUS * per
    first_y = jnp.where(lower, beyond, 0)
    first_f = jnp.where(lower, 0, beyond)
    first_1 = jnp.where(even, (RADIUS + 1) * per, (RADIUS - 1) * per)
    first_z = jnp.where(even, (RADIUS - 1) * per, (RADIUS + 1) * per)
    y_low, y_high = two(first_y)
    f_low, f_high = two(first_f)
    picks_ref[0] = y_low
    picks_ref[1] = y_high
    picks_ref[2] = f_low
    picks_ref[3] = f_high
    columns = [first_1 + j for j in range(per)] + [first_z + j for j in range(per)]
    columns += [first_y + y_low, first_y + y_high, first_f + f_low, first_f + f_high]
    for r in range(per):
        for n, c in enumerate(columns):
            value = jnp.where(mask_ref[r, c] > 0, 0.0, neg_large).astype(jnp.float32)
            bias_ref[r, :, n * BLOCK : (n + 1) * BLOCK] = jnp.full((1, BLOCK), value, jnp.float32)


def plan(place, block_mask):
    per = block_mask.shape[0]
    smem = pl.BlockSpec(memory_space=pltpu.SMEM)
    return pl.pallas_call(
        plan_kernel,
        in_specs=[smem, smem],
        out_specs=[smem, pl.BlockSpec(memory_space=pltpu.VMEM)],
        out_shape=[
            jax.ShapeDtypeStruct((4,), jnp.int32),
            jax.ShapeDtypeStruct((per, 1, 3 * per * BLOCK), jnp.float32),
        ],
        cost_estimate=CHEAP,
        name="plan",
    )(place, block_mask)


def attend_kernel(
    picks_ref, q_ref, k0_ref, v0_ref, k1_ref, v1_ref, near_ref, a_ref, b_ref, c_ref, d_ref, bias_ref, *rest
):
    o_ref = rest[-1]
    rows, size = q_ref.shape
    per = near_ref.shape[0]
    span = per * BLOCK
    near = near_ref[...]
    far = (a_ref, b_ref, c_ref, d_ref)
    keys = [
        k0_ref[...],
        k1_ref[...],
        near[:, 0].reshape(span, size),
        jnp.concatenate([r[0, 0] for r in far], axis=0),
    ]
    values = [
        v0_ref[...],
        v1_ref[...],
        near[:, 1].reshape(span, size),
        jnp.concatenate([r[0, 1] for r in far], axis=0),
    ]
    factor = math.log2(math.e) / math.sqrt(size)
    ones = jnp.ones((span, size), jnp.bfloat16)
    values = [jnp.concatenate([v, ones], axis=1) for v in values]

    def scores_of(m):
        q = q_ref[m * BLOCK : (m + 1) * BLOCK, :]
        scores, top = [], None
        for n, k in enumerate(keys):
            s = lax.dot_general(q, k, (((1,), (1,)), ((), ())), preferred_element_type=jnp.float32)
            if n:
                s = s + bias_ref[m, :, (n - 1) * span : n * span]
            scores.append(s)
            t = jnp.max(s, axis=1, keepdims=True)
            top = t if top is None else jnp.maximum(top, t)
        return scores, top

    def finish(m, scores, top):
        total = None
        for s, v in zip(scores, values):
            w = jnp.exp2((s - top) * factor).astype(jnp.bfloat16)
            part = jnp.dot(w, v, preferred_element_type=jnp.float32)
            total = part if total is None else total + part
        o_ref[m * BLOCK : (m + 1) * BLOCK, :] = (total[:, :size] / total[:, size:]).astype(o_ref.dtype)

    held = scores_of(0)
    for m in range(1, rows // BLOCK):
        ahead = scores_of(m)
        finish(m - 1, *held)
        held = ahead
    finish(rows // BLOCK - 1, *held)


def attend(first_head, per_part, picks, queries, key_rows, value_rows, core_k, core_v, near, y, z, bias, into):
    rows, width = queries.shape
    size = width // HEADS
    per = near.shape[0]
    flat = pl.BlockSpec((rows, size), lambda h, p: (0, first_head + h))
    far = [
        pl.BlockSpec((1, 2, BLOCK, size), lambda h, p, n=n: (p[n], 0, 0, h)) for n in range(4)
    ]
    in_specs = [
        flat,
        flat,
        flat,
        flat,
        flat,
        pl.BlockSpec((per, 2, BLOCK, size), lambda h, p: (0, 0, 0, h)),
        *far,
        pl.BlockSpec(bias.shape, lambda h, p: (0, 0, 0)),
    ]
    args = [queries, key_rows, value_rows, core_k, core_v, near, y, y, z, z, bias]
    aliases = {}
    if into is not None:
        in_specs.append(pl.BlockSpec(memory_space=pl.ANY))
        args.append(into)
        aliases = {len(args): 0}
    return pl.pallas_call(
        attend_kernel,
        grid_spec=pltpu.PrefetchScalarGridSpec(
            num_scalar_prefetch=1,
            grid=(per_part,),
            in_specs=in_specs,
            out_specs=flat,
        ),
        out_shape=jax.ShapeDtypeStruct((rows, width), jnp.bfloat16),
        input_output_aliases=aliases,
        compiler_params=pltpu.CompilerParams(vmem_limit_bytes=VMEM_LIMIT),
        cost_estimate=pl.CostEstimate(
            flops=ATTEND_FLOPS * per_part // 3, bytes_accessed=1000, transcendentals=0
        ),
        name="attend",
    )(picks, *args)


def project_kernel(place_ref, att_ref, *refs):
    *pieces, o_ref, held_ref = refs
    _, depth, cols = pieces[0].shape
    step = pl.program_id(0)

    @pl.when(step == 0)
    def _():
        for n in range(4):
            first = pl.multiple_of(place_ref[n] * depth, depth)
            held_ref[:, n * depth : (n + 1) * depth] = att_ref[:, pl.ds(first, depth)]

    def fill(half):
        own = jnp.concatenate([pieces[n][0] for n in range(4)], axis=0)
        other = jnp.concatenate([pieces[4 + 4 * half + n][0] for n in range(4)], axis=0)
        total = jnp.dot(
            held_ref[...], jnp.concatenate([own, other], axis=1), preferred_element_type=jnp.float32
        ).astype(o_ref.dtype)
        for f in range(2):
            to = pl.multiple_of(place_ref[4 + f] * cols, cols)
            o_ref[:, pl.ds(to, cols)] = total[:, f * cols : (f + 1) * cols]

    pl.when(step < 2)(lambda: fill(0))
    pl.when(step >= 2)(lambda: fill(1))


def project(places, attention, whole, halves):
    rows, width = attention.shape
    shifts, depth, cols = whole[0].shape
    size = (1, depth, cols)
    in_specs = [pl.BlockSpec((rows, width), lambda g, p: (0, 0))]
    in_specs += [pl.BlockSpec(size, lambda g, p: (g, 0, 0))] * 4
    in_specs += [pl.BlockSpec(size, lambda g, p: (jnp.minimum(g, 1), 0, 0))] * 4
    in_specs += [pl.BlockSpec(size, lambda g, p: (jnp.maximum(g - 2, 0), 0, 0))] * 4
    return pl.pallas_call(
        project_kernel,
        grid_spec=pltpu.PrefetchScalarGridSpec(
            num_scalar_prefetch=1,
            grid=(shifts,),
            in_specs=in_specs,
            out_specs=pl.BlockSpec((rows, 2 * cols), lambda g, p: (0, p[6 + g])),
            scratch_shapes=[pltpu.VMEM((rows, width), jnp.bfloat16)],
        ),
        out_shape=jax.ShapeDtypeStruct((rows, shifts * 2 * cols), jnp.bfloat16),
        compiler_params=pltpu.CompilerParams(vmem_limit_bytes=VMEM_LIMIT),
        cost_estimate=CHEAP,
        name="project",
    )(places, attention, *whole, *halves)


def local(groups, count, queries, key_rows, value_rows, block_mask, out_weight):
    tok_rows, feat_width = queries.shape
    per = tok_rows // BLOCK
    me = lax.axis_index("blk")
    place = me % 4
    up = lambda s: (s + 4) % count
    down = lambda s: (s - 4) % count
    over = lambda g, s: (1 - g, s)

    packs, first = [], 0
    for heads in PARTS:
        wide = heads * (feat_width // HEADS)
        k = key_rows[:, first : first + wide].reshape(per, 1, BLOCK, wide)
        v = value_rows[:, first : first + wide].reshape(per, 1, BLOCK, wide)
        packs.append(jnp.concatenate([k, v], axis=1))
        first += wide
    picks, bias = plan(place[None].astype(jnp.int32), block_mask)
    core_k = moved("core_keys", key_rows, other_core, count)
    core_v = moved("core_values", value_rows, other_core, count)

    special = SPECIAL and count == 16 and out_weight.shape[1] % 64 == 0
    if special:
        depth = out_weight.shape[0] // 4
        x = lax.axis_index("groups")
        core = me % 2
        own = lax.dynamic_slice_in_dim(out_weight, (x * 2 + core) * depth, depth, 0)
        give = lax.dynamic_slice_in_dim(out_weight, (x * 2 + 1 - core) * depth, depth, 0)
        got = moved("w_core", give, other_core, count)
        sides = [jnp.where(core == 0, own, got), jnp.where(core == 0, got, own)]
        piece = jnp.concatenate(sides, axis=1)
        own_up = moved("w_up", piece, up, count)
        own_down = moved("w_down", piece, down, count)
    outer = (place == 0) | (place == 3)

    def across_chips(n, *earlier):
        pack = after(packs[n], *earlier) if earlier else packs[n]
        return moved("kv_y%d" % n, pack, other_chip, count)

    def along_rows(n, y):
        return moved("kv_z%d" % n, y, next_row(count), count)

    def within_chip(n, y, z):
        return moved("kv_g%d" % n, jnp.where(outer, y, z), other_core, count)

    def attended(n, near, y, z, att):
        return attend(
            sum(PARTS[:n]), PARTS[n], picks, queries, key_rows, value_rows, core_k, core_v, near, y, z, bias, att
        )

    if special:
        t = place[None].astype(jnp.int32)
        y0 = across_chips(0)
        y1 = across_chips(1, piece)
        y2 = across_chips(2, piece)
        t = stepped(t, piece)
        t = stepped(t, after(core_k, t), after(core_v, t))
        core_k, core_v = after(core_k, t), after(core_v, t)
        t = stepped(t, after(own_up, t))
        own_up2 = moved("w_up2", after(own_up, t), up, count)
        t = stepped(t, after(own_down, t))
        t = stepped(t, after(y0, t))
        y0 = after(y0, t)
        z0 = along_rows(0, y0)
        t = stepped(t, after(own_up2, t))
        own_up, own_up2, own_down = after(own_up, t), after(own_up2, t), after(own_down, t)
        a1 = jnp.stack([piece, own_up, own_up2, own_down])
        a1x = jnp.stack([piece, own_up])
        a1y = jnp.stack([own_up2, own_down])
        b1 = moved_all("w_x1", a1, groups, count, over)
        a2x = moved("w_yx", a1x, other_chip, count)
        t = stepped(t, after(y1, t), a1, a1x)
        y1 = after(y1, t)
        z1 = along_rows(1, y1)
        y3 = across_chips(3, a1x)
        a2y = moved("w_yy", after(a1y, y1), other_chip, count)
        t = stepped(t, after(z0, t))
        z0 = after(z0, t)
        if EARLY:
            g0 = within_chip(0, y0, z0)
        t = stepped(t, after(y2, t))
        y2 = after(y2, t)
        if not EARLY:
            g0 = within_chip(0, y0, z0)
        z2 = along_rows(2, y2)
        if EARLY:
            att = attended(0, after(g0, t), y0, z0, None)
            t = stepped(t, after(z1, t), att)
        else:
            t = stepped(t, after(z1, t))
            att = attended(0, after(g0, t), y0, z0, None)
        z1 = after(z1, t)
        g1 = within_chip(1, y1, z1)
        t = stepped(t, after(y3, t), att)
        y3 = after(y3, t)
        z3 = along_rows(3, y3)
        t = stepped(t, after(a2x, t))
        a2x = after(a2x, t)
        b2x = moved_all("w_x2x", a2x, groups, count, over)
        t = stepped(t, after(b1, t))
        b1 = after(b1, t)
        c1 = moved("w_c1", after(a1, b1), other_core, count)
        d1 = moved("w_d1", b1, other_core, count)
        att = attended(1, after(g1, t), y1, z1, att)
        t = stepped(t, after(z2, t), att)
        z2 = after(z2, t)
        g2 = within_chip(2, y2, z2)
        t = stepped(t, after(a2y, t))
        a2y = after(a2y, t)
        b2y = moved_all("w_x2y", a2y, groups, count, over)
        t = stepped(t, after(b2x, t))
        d2x = moved("w_d2x", after(b2x, t), other_core, count)
        c2x = moved("w_c2x", after(a2x, t), other_core, count)
        att = attended(2, after(g2, t), y2, z2, att)
        t = stepped(t, after(z3, t, att))
        z3 = after(z3, t)
        g3 = within_chip(3, y3, z3)
        c2y = moved("w_c2y", after(a2y, t), other_core, count)
        t = stepped(t, after(b2y, t))
        d2y = moved("w_d2y", after(b2y, t), other_core, count)
        att = attended(3, g3, y3, z3, att)
    else:
        att = None
        for n in range(len(PARTS)):
            y = across_chips(n)
            z = along_rows(n, y)
            att = attended(n, within_chip(n, y, z), y, z, att)
    if special:
        z, y = me // 4, me // 2 % 2
        places = [x * 2 + core, (1 - x) * 2 + core, x * 2 + 1 - core, (1 - x) * 2 + 1 - core, y, 1 - y]
        places += [(z - shift) % (count // 4) for shift in range(count // 4)]
        whole = (a1, b1, c1, d1)
        halves = (a2x, b2x, c2x, d2x, a2y, b2y, c2y, d2y)
        return project(jnp.stack(places).astype(jnp.int32), att, whole, halves)
    full = lax.all_gather(out_weight, "blk", axis=1, tiled=True)
    return jnp.dot(att, full, preferred_element_type=jnp.float32).astype(jnp.bfloat16)


def solution(mesh):
    groups, count = mesh.shape["groups"], mesh.shape["blk"]
    in_specs = (
        P(("groups", "blk"), None),
        P(("groups", "blk"), None),
        P(("groups", "blk"), None),
        P("blk", None),
        P(None, "blk"),
    )
    out_specs = P(("groups", "blk"), None)

    def run(*args):
        return local(groups, count, *args)

    return jax.shard_map(run, mesh=mesh, in_specs=in_specs, out_specs=out_specs, check_vma=False)
```

```python
import math

import jax
import jax.numpy as jnp
from jax import lax
from jax.experimental import pallas as pl
from jax.experimental.pallas import tpu as pltpu
from jax.sharding import PartitionSpec as P

HEADS = 12
BLOCK = 128
RADIUS = 2
PARTS = (2,4,4,2)
W_A, W_B, W_C = 1, 2, 3
SPECIAL = True

neg_large = -1e30
VMEM_LIMIT = 60 * 1024 * 1024
STEP_FLOPS = 6_000_000_000
EARLY = False
ATTEND_FLOPS = 1_000_000_000
CHEAP = pl.CostEstimate(flops=1000, bytes_accessed=1000, transcendentals=0)


def moved(name, value, dest, count):
    with jax.named_scope(name):
        return lax.ppermute(value, "blk", [(s, dest(s)) for s in range(count)])


def moved_all(name, value, groups, count, dest):
    pairs = []
    for g in range(groups):
        for s in range(count):
            tg, ts = dest(g, s)
            pairs.append((g * count + s, tg * count + ts))
    with jax.named_scope(name):
        return lax.ppermute(value, ("groups", "blk"), pairs)


def after(value, *earlier):
    return lax.optimization_barrier((value, *earlier))[0]


def other_core(s):
    return s ^ 1


def other_chip(s):
    return s ^ 2


def next_row(count):
    return lambda s: (s + (4 if s % 4 < 2 else -4)) % count


def step_kernel(last_ref, *refs):
    refs[-1][0] = last_ref[0] + 1


def stepped(last, *arrived, weight=STEP_FLOPS):
    smem = pl.BlockSpec(memory_space=pltpu.SMEM)
    return pl.pallas_call(
        step_kernel,
        in_specs=[smem] + [pl.BlockSpec(memory_space=pl.ANY)] * len(arrived),
        out_specs=smem,
        out_shape=jax.ShapeDtypeStruct((1,), jnp.int32),
        cost_estimate=pl.CostEstimate(flops=weight, bytes_accessed=1000, transcendentals=0),
        name="step",
    )(last, *arrived)


def plan_kernel(place_ref, mask_ref, picks_ref, bias_ref):
    place = place_ref[0]
    per = mask_ref.shape[0]
    lower, even = place < 2, lax.rem(place, 2) == 0

    def two(first):
        used = []
        for j in range(per):
            u = mask_ref[0, first + j]
            for r in range(1, per):
                u = jnp.maximum(u, mask_ref[r, first + j])
            used.append(u)
        low, high = per - 1, 0
        for j in range(per):
            high = jnp.where(used[j] > 0, j, high)
            low = jnp.where(used[per - 1 - j] > 0, per - 1 - j, low)
        return low, high

    beyond = 2 * RADIUS * per
    first_y = jnp.where(lower, beyond, 0)
    first_f = jnp.where(lower, 0, beyond)
    first_1 = jnp.where(even, (RADIUS + 1) * per, (RADIUS - 1) * per)
    first_z = jnp.where(even, (RADIUS - 1) * per, (RADIUS + 1) * per)
    y_low, y_high = two(first_y)
    f_low, f_high = two(first_f)
    picks_ref[0] = y_low
    picks_ref[1] = y_high
    picks_ref[2] = f_low
    picks_ref[3] = f_high
    columns = [first_1 + j for j in range(per)] + [first_z + j for j in range(per)]
    columns += [first_y + y_low, first_y + y_high, first_f + f_low, first_f + f_high]
    for r in range(per):
        for n, c in enumerate(columns):
            value = jnp.where(mask_ref[r, c] > 0, 0.0, neg_large).astype(jnp.float32)
            bias_ref[r, :, n * BLOCK : (n + 1) * BLOCK] = jnp.full((1, BLOCK), value, jnp.float32)


def plan(place, block_mask):
    per = block_mask.shape[0]
    smem = pl.BlockSpec(memory_space=pltpu.SMEM)
    return pl.pallas_call(
        plan_kernel,
        in_specs=[smem, smem],
        out_specs=[smem, pl.BlockSpec(memory_space=pltpu.VMEM)],
        out_shape=[
            jax.ShapeDtypeStruct((4,), jnp.int32),
            jax.ShapeDtypeStruct((per, 1, 3 * per * BLOCK), jnp.float32),
        ],
        cost_estimate=CHEAP,
        name="plan",
    )(place, block_mask)


PAIR = 2


def attend_kernel(
    picks_ref, q_ref, k0_ref, v0_ref, k1_ref, v1_ref, near_ref, a_ref, b_ref, c_ref, d_ref, bias_ref, *rest
):
    o_ref = rest[-1]
    rows, size = q_ref.shape[0], q_ref.shape[1] // PAIR
    per = near_ref.shape[0]
    span = per * BLOCK
    far = (a_ref, b_ref, c_ref, d_ref)
    factor = math.log2(math.e) / math.sqrt(size)
    ones = jnp.ones((span, size), jnp.bfloat16)
    keys, values = [], []
    for head in range(PAIR):
        cols = slice(head * size, (head + 1) * size)
        near = near_ref[:, :, :, cols]
        keys.append([
            k0_ref[:, cols],
            k1_ref[:, cols],
            near[:, 0].reshape(span, size),
            jnp.concatenate([r[0, 0, :, cols] for r in far], axis=0),
        ])
        own = [
            v0_ref[:, cols],
            v1_ref[:, cols],
            near[:, 1].reshape(span, size),
            jnp.concatenate([r[0, 1, :, cols] for r in far], axis=0),
        ]
        values.append([jnp.concatenate([v, ones], axis=1) for v in own])

    def scores_of(head, m):
        q = q_ref[m * BLOCK : (m + 1) * BLOCK, head * size : (head + 1) * size]
        scores, top = [], None
        for n, k in enumerate(keys[head]):
            s = lax.dot_general(q, k, (((1,), (1,)), ((), ())), preferred_element_type=jnp.float32)
            if n:
                s = s + bias_ref[m, :, (n - 1) * span : n * span]
            scores.append(s)
            t = jnp.max(s, axis=1, keepdims=True)
            top = t if top is None else jnp.maximum(top, t)
        return scores, top

    def finish(head, m, scores, top):
        total = None
        for s, v in zip(scores, values[head]):
            w = jnp.exp2((s - top) * factor).astype(jnp.bfloat16)
            part = jnp.dot(w, v, preferred_element_type=jnp.float32)
            total = part if total is None else total + part
        o_ref[m * BLOCK : (m + 1) * BLOCK, head * size : (head + 1) * size] = (
            total[:, :size] / total[:, size:]
        ).astype(o_ref.dtype)

    blocks = [(head, m) for head in range(PAIR) for m in range(rows // BLOCK)]
    held = scores_of(*blocks[0])
    for block, following in zip(blocks, blocks[1:]):
        ahead = scores_of(*following)
        finish(*block, *held)
        held = ahead
    finish(*blocks[-1], *held)


def attend(first_head, per_part, picks, queries, key_rows, value_rows, core_k, core_v, near, y, z, bias, into):
    rows, width = queries.shape
    wide = width // HEADS * PAIR
    per = near.shape[0]
    flat = pl.BlockSpec((rows, wide), lambda h, p: (0, first_head // PAIR + h))
    far = [
        pl.BlockSpec((1, 2, BLOCK, wide), lambda h, p, n=n: (p[n], 0, 0, h)) for n in range(4)
    ]
    in_specs = [
        flat,
        flat,
        flat,
        flat,
        flat,
        pl.BlockSpec((per, 2, BLOCK, wide), lambda h, p: (0, 0, 0, h)),
        *far,
        pl.BlockSpec(bias.shape, lambda h, p: (0, 0, 0)),
    ]
    args = [queries, key_rows, value_rows, core_k, core_v, near, y, y, z, z, bias]
    aliases = {}
    if into is not None:
        in_specs.append(pl.BlockSpec(memory_space=pl.ANY))
        args.append(into)
        aliases = {len(args): 0}
    return pl.pallas_call(
        attend_kernel,
        grid_spec=pltpu.PrefetchScalarGridSpec(
            num_scalar_prefetch=1,
            grid=(per_part // PAIR,),
            in_specs=in_specs,
            out_specs=flat,
        ),
        out_shape=jax.ShapeDtypeStruct((rows, width), jnp.bfloat16),
        input_output_aliases=aliases,
        compiler_params=pltpu.CompilerParams(vmem_limit_bytes=VMEM_LIMIT),
        cost_estimate=pl.CostEstimate(
            flops=ATTEND_FLOPS * per_part // 3, bytes_accessed=1000, transcendentals=0
        ),
        name="attend",
    )(picks, *args)


def project_kernel(place_ref, att_ref, *refs):
    *pieces, o_ref, held_ref, w_ref, out_ref, att_sems, w_sems, out_sems = refs
    shifts, _, wide = w_ref.shape
    depth, cols = held_ref.shape[1] // 4, wide // 2
    ahead = 1

    def source(shift, flip, quarter):
        if flip == 0:
            return pieces[quarter].at[shift]
        return pieces[4 + 4 * (shift // 2) + quarter].at[shift % 2]

    att_copies = [
        pltpu.make_async_copy(
            att_ref.at[:, pl.ds(pl.multiple_of(place_ref[n] * depth, depth), depth)],
            held_ref.at[:, pl.ds(n * depth, depth)],
            att_sems.at[n],
        )
        for n in range(4)
    ]
    w_copies = [
        [
            pltpu.make_async_copy(
                source(shift, flip, n),
                w_ref.at[shift, pl.ds(n * depth, depth), pl.ds(flip * cols, cols)],
                w_sems.at[shift, flip * 4 + n],
            )
            for flip in range(2)
            for n in range(4)
        ]
        for shift in range(shifts)
    ]
    for copy in att_copies:
        copy.start()
    for copies in w_copies[:ahead]:
        for copy in copies:
            copy.start()
    for copy in att_copies:
        copy.wait()
    out_copies = []
    for shift in range(shifts):
        for copy in w_copies[shift]:
            copy.wait()
        if shift + ahead < shifts:
            for copy in w_copies[shift + ahead]:
                copy.start()
        half = held_ref.shape[0] // 2
        for m in range(2):
            mine = slice(m * half, (m + 1) * half)
            out_ref[shift, mine, :] = jnp.dot(
                held_ref[mine, :], w_ref[shift], preferred_element_type=jnp.float32
            ).astype(o_ref.dtype)
        for flip in range(2):
            to = pl.multiple_of((place_ref[6 + shift] * 2 + place_ref[4 + flip]) * cols, cols)
            copy = pltpu.make_async_copy(
                out_ref.at[shift, :, pl.ds(flip * cols, cols)],
                o_ref.at[:, pl.ds(to, cols)],
                out_sems.at[shift, flip],
            )
            copy.start()
            out_copies.append(copy)
    for copy in out_copies:
        copy.wait()


def project(places, attention, whole, halves):
    rows, width = attention.shape
    shifts, depth, cols = whole[0].shape
    anywhere = pl.BlockSpec(memory_space=pl.ANY)
    return pl.pallas_call(
        project_kernel,
        in_specs=[pl.BlockSpec(memory_space=pltpu.SMEM)] + [anywhere] * 13,
        out_specs=anywhere,
        out_shape=jax.ShapeDtypeStruct((rows, shifts * 2 * cols), jnp.bfloat16),
        scratch_shapes=[
            pltpu.VMEM((rows, width), jnp.bfloat16),
            pltpu.VMEM((shifts, width, 2 * cols), jnp.bfloat16),
            pltpu.VMEM((shifts, rows, 2 * cols), jnp.bfloat16),
            pltpu.SemaphoreType.DMA((4,)),
            pltpu.SemaphoreType.DMA((shifts, 8)),
            pltpu.SemaphoreType.DMA((shifts, 2)),
        ],
        compiler_params=pltpu.CompilerParams(vmem_limit_bytes=VMEM_LIMIT),
        cost_estimate=CHEAP,
        name="project",
    )(places, attention, *whole, *halves)


def local(groups, count, queries, key_rows, value_rows, block_mask, out_weight):
    tok_rows, feat_width = queries.shape
    per = tok_rows // BLOCK
    me = lax.axis_index("blk")
    place = me % 4
    up = lambda s: (s + 4) % count
    down = lambda s: (s - 4) % count
    over = lambda g, s: (1 - g, s)

    packs, first = [], 0
    for heads in PARTS:
        wide = heads * (feat_width // HEADS)
        k = key_rows[:, first : first + wide].reshape(per, 1, BLOCK, wide)
        v = value_rows[:, first : first + wide].reshape(per, 1, BLOCK, wide)
        packs.append(jnp.concatenate([k, v], axis=1))
        first += wide
    picks, bias = plan(place[None].astype(jnp.int32), block_mask)
    core_k = moved("core_keys", key_rows, other_core, count)
    core_v = moved("core_values", value_rows, other_core, count)

    special = SPECIAL and count == 16 and out_weight.shape[1] % 64 == 0
    if special:
        depth = out_weight.shape[0] // 4
        x = lax.axis_index("groups")
        core = me % 2
        own = lax.dynamic_slice_in_dim(out_weight, (x * 2 + core) * depth, depth, 0)
        give = lax.dynamic_slice_in_dim(out_weight, (x * 2 + 1 - core) * depth, depth, 0)
        got = moved("w_core", give, other_core, count)
        sides = [jnp.where(core == 0, own, got), jnp.where(core == 0, got, own)]
        piece = jnp.concatenate(sides, axis=1)
        own_up = moved("w_up", piece, up, count)
        own_down = moved("w_down", piece, down, count)
    outer = (place == 0) | (place == 3)

    def across_chips(n, *earlier):
        pack = after(packs[n], *earlier) if earlier else packs[n]
        return moved("kv_y%d" % n, pack, other_chip, count)

    def along_rows(n, y):
        return moved("kv_z%d" % n, y, next_row(count), count)

    def within_chip(n, y, z):
        return moved("kv_g%d" % n, jnp.where(outer, y, z), other_core, count)

    def attended(n, near, y, z, att):
        return attend(
            sum(PARTS[:n]), PARTS[n], picks, queries, key_rows, value_rows, core_k, core_v, near, y, z, bias, att
        )

    if special:
        t = place[None].astype(jnp.int32)
        y0 = across_chips(0)
        y1 = across_chips(1, piece)
        y2 = across_chips(2, piece)
        t = stepped(t, piece)
        t = stepped(t, after(core_k, t), after(core_v, t))
        core_k, core_v = after(core_k, t), after(core_v, t)
        t = stepped(t, after(own_up, t))
        own_up2 = moved("w_up2", after(own_up, t), up, count)
        t = stepped(t, after(own_down, t))
        t = stepped(t, after(y0, t))
        y0 = after(y0, t)
        z0 = along_rows(0, y0)
        t = stepped(t, after(own_up2, t))
        own_up, own_up2, own_down = after(own_up, t), after(own_up2, t), after(own_down, t)
        a1 = jnp.stack([piece, own_up, own_up2, own_down])
        a1x = jnp.stack([piece, own_up])
        a1y = jnp.stack([own_up2, own_down])
        b1 = moved_all("w_x1", a1, groups, count, over)
        a2x = moved("w_yx", a1x, other_chip, count)
        t = stepped(t, after(y1, t), a1, a1x)
        y1 = after(y1, t)
        z1 = along_rows(1, y1)
        y3 = across_chips(3, a1x)
        a2y = moved("w_yy", after(a1y, y1), other_chip, count)
        t = stepped(t, after(z0, t))
        z0 = after(z0, t)
        if EARLY:
            g0 = within_chip(0, y0, z0)
        t = stepped(t, after(y2, t))
        y2 = after(y2, t)
        if not EARLY:
            g0 = within_chip(0, y0, z0)
        z2 = along_rows(2, y2)
        if EARLY:
            att = attended(0, after(g0, t), y0, z0, None)
            t = stepped(t, after(z1, t), att)
        else:
            t = stepped(t, after(z1, t))
            att = attended(0, after(g0, t), y0, z0, None)
        z1 = after(z1, t)
        g1 = within_chip(1, y1, z1)
        t = stepped(t, after(y3, t), att)
        y3 = after(y3, t)
        z3 = along_rows(3, y3)
        t = stepped(t, after(a2x, t))
        a2x = after(a2x, t)
        b2x = moved_all("w_x2x", a2x, groups, count, over)
        t = stepped(t, after(b1, t))
        b1 = after(b1, t)
        c1 = moved("w_c1", after(a1, b1), other_core, count)
        d1 = moved("w_d1", b1, other_core, count)
        att = attended(1, after(g1, t), y1, z1, att)
        t = stepped(t, after(z2, t), att)
        z2 = after(z2, t)
        g2 = within_chip(2, y2, z2)
        t = stepped(t, after(a2y, t))
        a2y = after(a2y, t)
        b2y = moved_all("w_x2y", a2y, groups, count, over)
        t = stepped(t, after(b2x, t))
        d2x = moved("w_d2x", after(b2x, t), other_core, count)
        c2x = moved("w_c2x", after(a2x, t), other_core, count)
        att = attended(2, after(g2, t), y2, z2, att)
        t = stepped(t, after(z3, t, att))
        z3 = after(z3, t)
        g3 = within_chip(3, y3, z3)
        c2y = moved("w_c2y", after(a2y, t), other_core, count)
        t = stepped(t, after(b2y, t))
        d2y = moved("w_d2y", after(b2y, t), other_core, count)
        att = attended(3, g3, y3, z3, att)
    else:
        att = None
        for n in range(len(PARTS)):
            y = across_chips(n)
            z = along_rows(n, y)
            att = attended(n, within_chip(n, y, z), y, z, att)
    if special:
        z, y = me // 4, me // 2 % 2
        places = [x * 2 + core, (1 - x) * 2 + core, x * 2 + 1 - core, (1 - x) * 2 + 1 - core, y, 1 - y]
        places += [(z - shift) % (count // 4) for shift in range(count // 4)]
        whole = (a1, b1, c1, d1)
        halves = (a2x, b2x, c2x, d2x, a2y, b2y, c2y, d2y)
        return project(jnp.stack(places).astype(jnp.int32), att, whole, halves)
    full = lax.all_gather(out_weight, "blk", axis=1, tiled=True)
    return jnp.dot(att, full, preferred_element_type=jnp.float32).astype(jnp.bfloat16)


def solution(mesh):
    groups, count = mesh.shape["groups"], mesh.shape["blk"]
    in_specs = (
        P(("groups", "blk"), None),
        P(("groups", "blk"), None),
        P(("groups", "blk"), None),
        P("blk", None),
        P(None, "blk"),
    )
    out_specs = P(("groups", "blk"), None)

    def run(*args):
        return local(groups, count, *args)

    return jax.shard_map(run, mesh=mesh, in_specs=in_specs, out_specs=out_specs, check_vma=False)
```

```python
import math

import jax
import jax.numpy as jnp
from jax import lax
from jax.experimental import pallas as pl
from jax.experimental.pallas import tpu as pltpu
from jax.sharding import PartitionSpec as P

HEADS = 12
BLOCK = 128
RADIUS = 2
PARTS = (2,4,4,2)
W_A, W_B, W_C = 1, 2, 3
SPECIAL = True

neg_large = -1e30
VMEM_LIMIT = 60 * 1024 * 1024
STEP_FLOPS = 6_000_000_000
EARLY = False
ATTEND_FLOPS = 1_000_000_000
CHEAP = pl.CostEstimate(flops=1000, bytes_accessed=1000, transcendentals=0)


def moved(name, value, dest, count):
    with jax.named_scope(name):
        return lax.ppermute(value, "blk", [(s, dest(s)) for s in range(count)])


def moved_all(name, value, groups, count, dest):
    pairs = []
    for g in range(groups):
        for s in range(count):
            tg, ts = dest(g, s)
            pairs.append((g * count + s, tg * count + ts))
    with jax.named_scope(name):
        return lax.ppermute(value, ("groups", "blk"), pairs)


def after(value, *earlier):
    return lax.optimization_barrier((value, *earlier))[0]


def other_core(s):
    return s ^ 1


def other_chip(s):
    return s ^ 2


def next_row(count):
    return lambda s: (s + (4 if s % 4 < 2 else -4)) % count


def step_kernel(last_ref, *refs):
    refs[-1][0] = last_ref[0] + 1


def stepped(last, *arrived, weight=STEP_FLOPS):
    smem = pl.BlockSpec(memory_space=pltpu.SMEM)
    return pl.pallas_call(
        step_kernel,
        in_specs=[smem] + [pl.BlockSpec(memory_space=pl.ANY)] * len(arrived),
        out_specs=smem,
        out_shape=jax.ShapeDtypeStruct((1,), jnp.int32),
        cost_estimate=pl.CostEstimate(flops=weight, bytes_accessed=1000, transcendentals=0),
        name="step",
    )(last, *arrived)


def plan_kernel(place_ref, mask_ref, picks_ref, bias_ref):
    place = place_ref[0]
    per = mask_ref.shape[0]
    lower, even = place < 2, lax.rem(place, 2) == 0

    def two(first):
        used = []
        for j in range(per):
            u = mask_ref[0, first + j]
            for r in range(1, per):
                u = jnp.maximum(u, mask_ref[r, first + j])
            used.append(u)
        low, high = per - 1, 0
        for j in range(per):
            high = jnp.where(used[j] > 0, j, high)
            low = jnp.where(used[per - 1 - j] > 0, per - 1 - j, low)
        return low, high

    beyond = 2 * RADIUS * per
    first_y = jnp.where(lower, beyond, 0)
    first_f = jnp.where(lower, 0, beyond)
    first_1 = jnp.where(even, (RADIUS + 1) * per, (RADIUS - 1) * per)
    first_z = jnp.where(even, (RADIUS - 1) * per, (RADIUS + 1) * per)
    y_low, y_high = two(first_y)
    f_low, f_high = two(first_f)
    picks_ref[0] = y_low
    picks_ref[1] = y_high
    picks_ref[2] = f_low
    picks_ref[3] = f_high
    columns = [first_1 + j for j in range(per)] + [first_z + j for j in range(per)]
    columns += [first_y + y_low, first_y + y_high, first_f + f_low, first_f + f_high]
    for r in range(per):
        for n, c in enumerate(columns):
            value = jnp.where(mask_ref[r, c] > 0, 0.0, neg_large).astype(jnp.float32)
            bias_ref[r, :, n * BLOCK : (n + 1) * BLOCK] = jnp.full((1, BLOCK), value, jnp.float32)


def plan(place, block_mask):
    per = block_mask.shape[0]
    smem = pl.BlockSpec(memory_space=pltpu.SMEM)
    return pl.pallas_call(
        plan_kernel,
        in_specs=[smem, smem],
        out_specs=[smem, pl.BlockSpec(memory_space=pltpu.VMEM)],
        out_shape=[
            jax.ShapeDtypeStruct((4,), jnp.int32),
            jax.ShapeDtypeStruct((per, 1, 3 * per * BLOCK), jnp.float32),
        ],
        cost_estimate=CHEAP,
        name="plan",
    )(place, block_mask)


PAIR = 2


def attend_kernel(
    picks_ref, q_ref, k0_ref, v0_ref, k1_ref, v1_ref, near_ref, a_ref, b_ref, c_ref, d_ref, bias_ref, *rest
):
    o_ref = rest[-1]
    rows, size = q_ref.shape[0], q_ref.shape[1] // PAIR
    per = near_ref.shape[0]
    span = per * BLOCK
    far = (a_ref, b_ref, c_ref, d_ref)
    factor = math.log2(math.e) / math.sqrt(size)
    ones = jnp.ones((span, size), jnp.bfloat16)
    keys, values = [], []
    for head in range(PAIR):
        cols = slice(head * size, (head + 1) * size)
        near = near_ref[:, :, :, cols]
        keys.append([
            k0_ref[:, cols],
            k1_ref[:, cols],
            near[:, 0].reshape(span, size),
            jnp.concatenate([r[0, 0, :, cols] for r in far], axis=0),
        ])
        own = [
            v0_ref[:, cols],
            v1_ref[:, cols],
            near[:, 1].reshape(span, size),
            jnp.concatenate([r[0, 1, :, cols] for r in far], axis=0),
        ]
        values.append([jnp.concatenate([v, ones], axis=1) for v in own])

    def scores_of(head, m):
        q = q_ref[m * BLOCK : (m + 1) * BLOCK, head * size : (head + 1) * size]
        scores, top = [], None
        for n, k in enumerate(keys[head]):
            s = lax.dot_general(q, k, (((1,), (1,)), ((), ())), preferred_element_type=jnp.float32)
            if n:
                s = s + bias_ref[m, :, (n - 1) * span : n * span]
            scores.append(s)
            t = jnp.max(s, axis=1, keepdims=True)
            top = t if top is None else jnp.maximum(top, t)
        return scores, top

    def finish(head, m, scores, top):
        total = None
        for s, v in zip(scores, values[head]):
            w = jnp.exp2((s - top) * factor).astype(jnp.bfloat16)
            part = jnp.dot(w, v, preferred_element_type=jnp.float32)
            total = part if total is None else total + part
        o_ref[m * BLOCK : (m + 1) * BLOCK, head * size : (head + 1) * size] = (
            total[:, :size] / total[:, size:]
        ).astype(o_ref.dtype)

    blocks = [(head, m) for head in range(PAIR) for m in range(rows // BLOCK)]
    held = scores_of(*blocks[0])
    for block, following in zip(blocks, blocks[1:]):
        ahead = scores_of(*following)
        finish(*block, *held)
        held = ahead
    finish(*blocks[-1], *held)


def attend(first_head, per_part, picks, queries, key_rows, value_rows, core_k, core_v, near, y, z, bias, into):
    rows, width = queries.shape
    wide = width // HEADS * PAIR
    per = near.shape[0]
    flat = pl.BlockSpec((rows, wide), lambda h, p: (0, first_head // PAIR + h))
    far = [
        pl.BlockSpec((1, 2, BLOCK, wide), lambda h, p, n=n: (p[n], 0, 0, h)) for n in range(4)
    ]
    in_specs = [
        flat,
        flat,
        flat,
        flat,
        flat,
        pl.BlockSpec((per, 2, BLOCK, wide), lambda h, p: (0, 0, 0, h)),
        *far,
        pl.BlockSpec(bias.shape, lambda h, p: (0, 0, 0)),
    ]
    args = [queries, key_rows, value_rows, core_k, core_v, near, y, y, z, z, bias]
    aliases = {}
    if into is not None:
        in_specs.append(pl.BlockSpec(memory_space=pl.ANY))
        args.append(into)
        aliases = {len(args): 0}
    return pl.pallas_call(
        attend_kernel,
        grid_spec=pltpu.PrefetchScalarGridSpec(
            num_scalar_prefetch=1,
            grid=(per_part // PAIR,),
            in_specs=in_specs,
            out_specs=flat,
        ),
        out_shape=jax.ShapeDtypeStruct((rows, width), jnp.bfloat16),
        input_output_aliases=aliases,
        compiler_params=pltpu.CompilerParams(vmem_limit_bytes=VMEM_LIMIT),
        cost_estimate=pl.CostEstimate(
            flops=ATTEND_FLOPS * per_part // 3, bytes_accessed=1000, transcendentals=0
        ),
        name="attend",
    )(picks, *args)


def project_kernel(place_ref, att_ref, *refs):
    *pieces, o_ref, held_ref, w_ref, out_ref, att_sems, w_sems, out_sems = refs
    shifts, _, wide = w_ref.shape
    depth, cols = held_ref.shape[1] // 4, wide // 2
    ahead = 1

    def source(shift, flip, quarter):
        if flip == 0:
            return pieces[quarter].at[shift]
        return pieces[4 + 4 * (shift // 2) + quarter].at[shift % 2]

    att_copies = [
        pltpu.make_async_copy(
            att_ref.at[:, pl.ds(pl.multiple_of(place_ref[n] * depth, depth), depth)],
            held_ref.at[:, pl.ds(n * depth, depth)],
            att_sems.at[n],
        )
        for n in range(4)
    ]
    w_copies = [
        [
            pltpu.make_async_copy(
                source(shift, flip, n),
                w_ref.at[shift, pl.ds(n * depth, depth), pl.ds(flip * cols, cols)],
                w_sems.at[shift, flip * 4 + n],
            )
            for flip in range(2)
            for n in range(4)
        ]
        for shift in range(shifts)
    ]
    for copy in att_copies:
        copy.start()
    for copies in w_copies[:ahead]:
        for copy in copies:
            copy.start()
    for copy in att_copies:
        copy.wait()
    out_copies = []
    for shift in range(shifts):
        for copy in w_copies[shift]:
            copy.wait()
        if shift + ahead < shifts:
            for copy in w_copies[shift + ahead]:
                copy.start()
        half = held_ref.shape[0] // 2
        for m in range(2):
            mine = slice(m * half, (m + 1) * half)
            out_ref[shift, mine, :] = jnp.dot(
                held_ref[mine, :], w_ref[shift], preferred_element_type=jnp.float32
            ).astype(o_ref.dtype)
            for flip in range(2):
                to = pl.multiple_of((place_ref[6 + shift] * 2 + place_ref[4 + flip]) * cols, cols)
                copy = pltpu.make_async_copy(
                    out_ref.at[shift, pl.ds(m * half, half), pl.ds(flip * cols, cols)],
                    o_ref.at[pl.ds(m * half, half), pl.ds(to, cols)],
                    out_sems.at[shift, m * 2 + flip],
                )
                copy.start()
                out_copies.append(copy)
    for copy in out_copies:
        copy.wait()


def project(places, attention, whole, halves):
    rows, width = attention.shape
    shifts, depth, cols = whole[0].shape
    anywhere = pl.BlockSpec(memory_space=pl.ANY)
    return pl.pallas_call(
        project_kernel,
        in_specs=[pl.BlockSpec(memory_space=pltpu.SMEM)] + [anywhere] * 13,
        out_specs=anywhere,
        out_shape=jax.ShapeDtypeStruct((rows, shifts * 2 * cols), jnp.bfloat16),
        scratch_shapes=[
            pltpu.VMEM((rows, width), jnp.bfloat16),
            pltpu.VMEM((shifts, width, 2 * cols), jnp.bfloat16),
            pltpu.VMEM((shifts, rows, 2 * cols), jnp.bfloat16),
            pltpu.SemaphoreType.DMA((4,)),
            pltpu.SemaphoreType.DMA((shifts, 8)),
            pltpu.SemaphoreType.DMA((shifts, 4)),
        ],
        compiler_params=pltpu.CompilerParams(vmem_limit_bytes=VMEM_LIMIT),
        cost_estimate=CHEAP,
        name="project",
    )(places, attention, *whole, *halves)


def local(groups, count, queries, key_rows, value_rows, block_mask, out_weight):
    tok_rows, feat_width = queries.shape
    per = tok_rows // BLOCK
    me = lax.axis_index("blk")
    place = me % 4
    up = lambda s: (s + 4) % count
    down = lambda s: (s - 4) % count
    over = lambda g, s: (1 - g, s)

    packs, first = [], 0
    for heads in PARTS:
        wide = heads * (feat_width // HEADS)
        k = key_rows[:, first : first + wide].reshape(per, 1, BLOCK, wide)
        v = value_rows[:, first : first + wide].reshape(per, 1, BLOCK, wide)
        packs.append(jnp.concatenate([k, v], axis=1))
        first += wide
    picks, bias = plan(place[None].astype(jnp.int32), block_mask)
    core_k = moved("core_keys", key_rows, other_core, count)
    core_v = moved("core_values", value_rows, other_core, count)

    special = SPECIAL and count == 16 and out_weight.shape[1] % 64 == 0
    if special:
        depth = out_weight.shape[0] // 4
        x = lax.axis_index("groups")
        core = me % 2
        own = lax.dynamic_slice_in_dim(out_weight, (x * 2 + core) * depth, depth, 0)
        give = lax.dynamic_slice_in_dim(out_weight, (x * 2 + 1 - core) * depth, depth, 0)
        got = moved("w_core", give, other_core, count)
        sides = [jnp.where(core == 0, own, got), jnp.where(core == 0, got, own)]
        piece = jnp.concatenate(sides, axis=1)
        own_up = moved("w_up", piece, up, count)
        own_down = moved("w_down", piece, down, count)
    outer = (place == 0) | (place == 3)

    def across_chips(n, *earlier):
        pack = after(packs[n], *earlier) if earlier else packs[n]
        return moved("kv_y%d" % n, pack, other_chip, count)

    def along_rows(n, y):
        return moved("kv_z%d" % n, y, next_row(count), count)

    def within_chip(n, y, z):
        return moved("kv_g%d" % n, jnp.where(outer, y, z), other_core, count)

    def attended(n, near, y, z, att):
        return attend(
            sum(PARTS[:n]), PARTS[n], picks, queries, key_rows, value_rows, core_k, core_v, near, y, z, bias, att
        )

    if special:
        t = place[None].astype(jnp.int32)
        y0 = across_chips(0)
        y1 = across_chips(1, piece)
        y2 = across_chips(2, piece)
        t = stepped(t, piece)
        t = stepped(t, after(core_k, t), after(core_v, t))
        core_k, core_v = after(core_k, t), after(core_v, t)
        t = stepped(t, after(own_up, t))
        own_up2 = moved("w_up2", after(own_up, t), up, count)
        t = stepped(t, after(own_down, t))
        t = stepped(t, after(y0, t))
        y0 = after(y0, t)
        z0 = along_rows(0, y0)
        t = stepped(t, after(own_up2, t))
        own_up, own_up2, own_down = after(own_up, t), after(own_up2, t), after(own_down, t)
        a1 = jnp.stack([piece, own_up, own_up2, own_down])
        a1x = jnp.stack([piece, own_up])
        a1y = jnp.stack([own_up2, own_down])
        b1 = moved_all("w_x1", a1, groups, count, over)
        a2x = moved("w_yx", a1x, other_chip, count)
        t = stepped(t, after(y1, t), a1, a1x)
        y1 = after(y1, t)
        z1 = along_rows(1, y1)
        y3 = across_chips(3, a1x)
        a2y = moved("w_yy", after(a1y, y1), other_chip, count)
        t = stepped(t, after(z0, t))
        z0 = after(z0, t)
        if EARLY:
            g0 = within_chip(0, y0, z0)
        t = stepped(t, after(y2, t))
        y2 = after(y2, t)
        if not EARLY:
            g0 = within_chip(0, y0, z0)
        z2 = along_rows(2, y2)
        if EARLY:
            att = attended(0, after(g0, t), y0, z0, None)
            t = stepped(t, after(z1, t), att)
        else:
            t = stepped(t, after(z1, t))
            att = attended(0, after(g0, t), y0, z0, None)
        z1 = after(z1, t)
        g1 = within_chip(1, y1, z1)
        t = stepped(t, after(y3, t), att)
        y3 = after(y3, t)
        z3 = along_rows(3, y3)
        t = stepped(t, after(a2x, t))
        a2x = after(a2x, t)
        b2x = moved_all("w_x2x", a2x, groups, count, over)
        t = stepped(t, after(b1, t))
        b1 = after(b1, t)
        c1 = moved("w_c1", after(a1, b1), other_core, count)
        d1 = moved("w_d1", b1, other_core, count)
        att = attended(1, after(g1, t), y1, z1, att)
        t = stepped(t, after(z2, t), att)
        z2 = after(z2, t)
        g2 = within_chip(2, y2, z2)
        t = stepped(t, after(a2y, t))
        a2y = after(a2y, t)
        b2y = moved_all("w_x2y", a2y, groups, count, over)
        t = stepped(t, after(b2x, t))
        d2x = moved("w_d2x", after(b2x, t), other_core, count)
        c2x = moved("w_c2x", after(a2x, t), other_core, count)
        att = attended(2, after(g2, t), y2, z2, att)
        t = stepped(t, after(z3, t, att))
        z3 = after(z3, t)
        g3 = within_chip(3, y3, z3)
        c2y = moved("w_c2y", after(a2y, t), other_core, count)
        t = stepped(t, after(b2y, t))
        d2y = moved("w_d2y", after(b2y, t), other_core, count)
        att = attended(3, g3, y3, z3, att)
    else:
        att = None
        for n in range(len(PARTS)):
            y = across_chips(n)
            z = along_rows(n, y)
            att = attended(n, within_chip(n, y, z), y, z, att)
    if special:
        z, y = me // 4, me // 2 % 2
        places = [x * 2 + core, (1 - x) * 2 + core, x * 2 + 1 - core, (1 - x) * 2 + 1 - core, y, 1 - y]
        places += [(z - shift) % (count // 4) for shift in range(count // 4)]
        whole = (a1, b1, c1, d1)
        halves = (a2x, b2x, c2x, d2x, a2y, b2y, c2y, d2y)
        return project(jnp.stack(places).astype(jnp.int32), att, whole, halves)
    full = lax.all_gather(out_weight, "blk", axis=1, tiled=True)
    return jnp.dot(att, full, preferred_element_type=jnp.float32).astype(jnp.bfloat16)


def solution(mesh):
    groups, count = mesh.shape["groups"], mesh.shape["blk"]
    in_specs = (
        P(("groups", "blk"), None),
        P(("groups", "blk"), None),
        P(("groups", "blk"), None),
        P("blk", None),
        P(None, "blk"),
    )
    out_specs = P(("groups", "blk"), None)

    def run(*args):
        return local(groups, count, *args)

    return jax.shard_map(run, mesh=mesh, in_specs=in_specs, out_specs=out_specs, check_vma=False)
```
